256 devices in a mesh: row: 32 (over y, x, core), col: 8 (over z).
Axes of the slice: x: 4, y: 4, z: 8, core: 2. Of those that a mesh axis runs over, the one named last changes fastest.
Arguments:
- grad: bfloat16 [8192, 26624], P('row', 'col'), may hold values from -6 to 6
- momentum: bfloat16 [8192, 26624], P('row', 'col'), may hold values from -6 to 6
- q_prev: float32 [26624, 128], P('col'), may hold values from -0.0390625 to 0.0390625
Outputs:
- momentum_new: bfloat16 [8192, 26624], P('row', 'col')
- direction: bfloat16 [8192, 26624], P('row', 'col')
- q_new: float32 [26624, 128], P('col')
The draws below stay inside these ranges and needn't reach their ends.
All inputs are finite; a program needn't handle non-finite values.
Results may differ from the reference program's by a relative error of at most 0.009.
Values may be sent and summed in bfloat16 or wider, within the bound.
A program may use at most 64 MiB of HBM per device.

```python
import math
import jax
import jax.numpy as jnp
from jax import lax

M = 8192
N = 26624
RANK = 128


def shard_levels(stream_key, extent, cuts, least, top_value):
    loudness = 1.0
    for position, blocks in cuts:
        steps = jax.random.uniform(jax.random.fold_in(jax.random.fold_in(stream_key, 6), position), (blocks,), jnp.float32, least / len(cuts), top_value / len(cuts))
        loudness = loudness * jnp.repeat(jnp.exp(steps), extent[position] // blocks).reshape((-1,) + (1,) * (len(extent) - 1 - position))
    return loudness


def noise(key, shape, width, bound, shards=(), held_as=jnp.bfloat16):
    level = shard_levels(key, shape, shards, -0.22, 0.18) if shards else 1.0
    entries = jax.random.normal(key, shape, jnp.float32) * width * level
    return jnp.minimum(jnp.maximum(entries, -bound), bound).astype(held_as)


def setup_inputs(seed: int = 0) -> dict:
    seeds = jax.random.split(jax.random.key(seed), 4)
    return {
        "grad": noise(seeds[0], (M, N), 1.0, 6.0, ((0, 32), (1, 8))),
        "momentum": noise(seeds[1], (M, N), 1.0, 6.0, ((0, 32), (1, 8))),
        "q_prev": noise(seeds[2], (N, RANK), N ** -0.5, 0.0390625, ((0, 8),), jnp.float32),
    }


momentum_keep = 0.9
epsilon = 1e-06

def reference(grad, momentum, q_prev):
    buffer = momentum_keep * momentum.astype(jnp.float32) + grad.astype(jnp.float32)
    buffer_b = buffer.astype(jnp.bfloat16)
    power = jnp.dot(buffer_b.astype(jnp.float32), q_prev.astype(jnp.bfloat16).astype(jnp.float32), preferred_element_type=jnp.float32)
    gram_matrix = jnp.dot(power.T, power, precision=lax.Precision.HIGHEST)
    lower = jnp.linalg.cholesky(gram_matrix)
    ortho = lax.linalg.triangular_solve(lower, power, left_side=False, lower=True, transpose_a=True)
    ortho_b = ortho.astype(jnp.bfloat16)
    factor = jnp.dot(buffer_b.T.astype(jnp.float32), ortho_b.astype(jnp.float32), preferred_element_type=jnp.float32)
    squares = lax.optimization_barrier(jnp.sum(factor * factor, axis=0))
    q_new = factor / jnp.sqrt(squares + epsilon)
    feedback = jnp.dot(ortho_b.astype(jnp.float32), factor.astype(jnp.bfloat16).T.astype(jnp.float32), preferred_element_type=jnp.float32)
    momentum_new = (buffer - (1.0 - momentum_keep) * feedback).astype(jnp.bfloat16)
    scaling = math.sqrt(M * N / RANK)
    direction = (scaling * jnp.dot(ortho_b.astype(jnp.float32), q_new.astype(jnp.bfloat16).T.astype(jnp.float32), preferred_element_type=jnp.float32)).astype(jnp.bfloat16)
    return (momentum_new, direction, q_new)
```

```python
import functools
import math

import jax
import jax.numpy as jnp
from jax import lax
from jax.experimental import pallas as pl
from jax.experimental.pallas import tpu as pltpu
from jax.sharding import PartitionSpec as P

momentum_keep = 0.9
epsilon = 1e-06
MESH = pl.DeviceIdType.MESH
HIGHEST = lax.Precision.HIGHEST
LANES = 128
Z = 8
CHIPS = 16


def remote(src, dst, send, recv, device):
    return pltpu.make_async_remote_copy(
        src_ref=src, dst_ref=dst, send_sem=send, recv_sem=recv, device_id=device, device_id_type=MESH
    )


def inverse_cholesky(a_ref):
    rank = a_ref.shape[0]
    lane = lax.broadcasted_iota(jnp.int32, (8, LANES), 1)
    sub = lax.broadcasted_iota(jnp.int32, (8, LANES), 0)
    lane_all = lax.broadcasted_iota(jnp.int32, (rank, LANES), 1)
    row_all = lax.broadcasted_iota(jnp.int32, (rank, LANES), 0)

    def block(b, _):
        rows = pl.ds(pl.multiple_of(b * 8, 8), 8)
        a = a_ref[...]
        r = a_ref[rows, :]
        cols = [jnp.broadcast_to(r[:, k : k + 1], (8, LANES)) for k in range(8)]
        q = jnp.where(lane < 8, 0.0, r)
        v = jnp.zeros((8, LANES), jnp.float32)
        pivots = jnp.zeros((8, LANES), jnp.float32)
        inverses = jnp.zeros((8, LANES), jnp.float32)
        for j in range(8):
            pivot = jnp.broadcast_to(cols[j][j : j + 1, :], (8, LANES))
            inv = 1.0 / pivot
            here = sub == j
            m = jnp.where(here, 0.0, cols[j] * inv)
            qj = jnp.broadcast_to(q[j : j + 1, :], (8, LANES)) + jnp.where(lane == j, 1.0, 0.0)
            pivots = jnp.where(here, pivot, pivots)
            inverses = jnp.where(here, inv, inverses)
            v = jnp.where(here, qj, v)
            q = jnp.where(here, qj, q - m * qj)
            for k in range(j + 1, 8):
                cols[k] = cols[k] - m * jnp.broadcast_to(cols[k][j : j + 1, :], (8, LANES))
        q = q * inverses
        new = jnp.where(lane_all < 8, 0.0, a)
        below = row_all >= b * 8 + 8
        total = jnp.zeros((rank, LANES), jnp.float32)
        for k in range(8):
            total = total + a[:, k : k + 1] * q[k : k + 1, :]
        new = jnp.where(below, new - total, new)
        a_ref[...] = pltpu.roll(new, LANES - 8, 1)
        a_ref[rows, :] = pltpu.roll(v * lax.rsqrt(pivots), LANES - 8, 1)
        return 0

    lax.fori_loop(0, rank // 8, block, 0)


NEAR = sorted(
    ((dy, dx) for dy in range(4) for dx in range(4) if (dy, dx) != (0, 0)),
    key=lambda d: min(d[0], 4 - d[0]) + min(d[1], 4 - d[1]),
)


def main_kernel(
    grad, mom, qprev, factor, ortho, sq, mnew,
    gbuf, mbuf, qbuf, buf, bb, pp, prs, pw, p3, pk, cg, gx, gs, amat, wt, wc, wr, fb, sz, sx, sc,
    in_sem, s1, r1, s2, r2, s3, r3, s4, r4, s5, r5, s6, r6, s7, r7, s8, r8, s9, r9, sf, s10, r10, s11, r11,
):
    rowi = lax.axis_index("row")
    c = lax.axis_index("col")
    chip = rowi // 2
    k = lax.rem(rowi, 2)
    other = 1 - k
    sibling = (chip * 2 + other, c)
    tiles = bb.shape[1] // LANES
    share = wr.shape[1]

    def zpeer(o):
        t = lax.rem(c + o, Z)
        return t, (rowi, t)

    def cpeer(d):
        t = lax.rem(chip // 4 + d[0], 4) * 4 + lax.rem(chip + d[1], 4)
        return t, (t * 2 + k, c)

    others = [cpeer(d) for d in NEAR]

    bounds = [0, 7, 14, 20, tiles]
    loads = []
    for i in range(4):
        lanes = pl.ds(bounds[i] * LANES, (bounds[i + 1] - bounds[i]) * LANES)
        part = [
            pltpu.make_async_copy(grad.at[:, lanes], gbuf.at[:, lanes], in_sem.at[i, 0]),
            pltpu.make_async_copy(mom.at[:, lanes], mbuf.at[:, lanes], in_sem.at[i, 1]),
            pltpu.make_async_copy(qprev.at[lanes, :], qbuf.at[lanes, :], in_sem.at[i, 2]),
        ]
        for copy in part:
            copy.start()
        loads.append(part)

    barrier = pltpu.get_barrier_semaphore()

    for o in range(1, Z):
        pl.semaphore_signal(barrier, inc=1, device_id=zpeer(o)[1], device_id_type=MESH)
    for _, dev in others:
        pl.semaphore_signal(barrier, inc=1, device_id=dev, device_id_type=MESH)
    pl.semaphore_signal(barrier, inc=1, device_id=sibling, device_id_type=MESH)

    rows = bb.shape[0]
    for i in range(4):
        for copy in loads[i]:
            copy.wait()
        lanes = pl.ds(bounds[i] * LANES, (bounds[i + 1] - bounds[i]) * LANES)

        def strip(s, _):
            rs = pl.ds(pl.multiple_of(s * 32, 32), 32)
            g = gbuf[rs, lanes].astype(jnp.float32)
            m = mbuf[rs, lanes].astype(jnp.float32)
            b = momentum_keep * m + g
            buf[rs, lanes] = b
            bb[rs, lanes] = b.astype(jnp.bfloat16)
            return 0

        lax.fori_loop(0, rows // 32, strip, 0)
        d = jnp.dot(bb[:, lanes], qbuf[lanes, :].astype(jnp.bfloat16), preferred_element_type=jnp.float32)
        d = d.reshape(Z, rows // Z, LANES)
        pp[...] = d if i == 0 else pp[...] + d

    pl.semaphore_wait(barrier, Z - 1 + CHIPS - 1 + 1)

    far_first = (4, 3, 5, 2, 6, 1, 7)
    sends = []
    for o in far_first:
        t, dev = zpeer(o)
        copy = remote(pp.at[t], prs.at[c], s1.at[o], r1.at[c], dev)
        copy.start()
        sends.append(copy)
    red = pp[c]
    for o in (1, 7, 2, 6, 3, 5, 4):
        s = lax.rem(c + o, Z)
        remote(pp.at[s], prs.at[s], s1.at[0], r1.at[s], sibling).wait_recv()
        red = red + prs[s]
    pw[c] = red
    for o in far_first:
        t, dev = zpeer(o)
        copy = remote(pw.at[c], pw.at[c], s2.at[o], r2.at[c], dev)
        copy.start()
        sends.append(copy)
    for o in (1, 7, 2, 6, 3, 5, 4):
        s = lax.rem(c + o, Z)
        remote(pw.at[s], pw.at[s], s2.at[0], r2.at[s], sibling).wait_recv()

    power = pw[...].reshape(rows, LANES)
    pt = power.T
    gram = jnp.dot(pt, power, precision=HIGHEST, preferred_element_type=jnp.float32)
    lane64 = lax.broadcasted_iota(jnp.int32, (64, LANES), 1)
    lane32 = lax.broadcasted_iota(jnp.int32, (32, LANES), 1)
    top, bottom = gram[:64], gram[64:]
    pk[0:64] = jnp.where(lane64 < 64, top, bottom)
    pk[64:96] = jnp.where(lane32 >= 64, top[:32], pltpu.roll(top[32:], 64, 1))
    mine = pl.ds(pl.multiple_of(k * 48, 16), 48)
    theirs = pl.ds(pl.multiple_of(other * 48, 16), 48)
    copy = remote(pk.at[theirs], cg, s3, r3, sibling)
    copy.start()
    sends.append(copy)

    hi = power.astype(jnp.bfloat16)
    rest = power - hi.astype(jnp.float32)
    mid = rest.astype(jnp.bfloat16)
    p3[:, 0:128] = hi
    p3[:, 128:256] = mid
    p3[:, 256:384] = (rest - mid.astype(jnp.float32)).astype(jnp.bfloat16)
    for i in range(4):
        cols = slice(bounds[i] * LANES, bounds[i + 1] * LANES)
        d = lax.dot_general(bb[:, cols], p3[...], (((0,), (0,)), ((), ())), preferred_element_type=jnp.float32)
        wt[cols, :] = d[:, 0:128] + (d[:, 128:256] + d[:, 256:384])

    def shares(u, core):
        return wt.at[pl.ds(pl.multiple_of((2 * u + core) * share, 8), share)]

    def exchange(u):
        return remote(shares(u, other), wc.at[u], s4.at[u], r4.at[u], sibling)

    for u, _ in others:
        exchange(u).start()
    exchange(chip).start()

    remote(cg, cg, s3, r3, sibling).wait_recv()
    gx[chip] = pk[mine] + cg[...]
    for i, (t, dev) in enumerate(others):
        copy = remote(gx.at[chip], gx.at[chip], s5.at[i], r5.at[chip], dev)
        copy.start()
        sends.append(copy)

    for i, (u, dev) in enumerate(others):
        exchange(u).wait_recv()
        wc[u] = wc[u] + shares(u, k)[...]
        copy = remote(wc.at[u], wr.at[chip], s6.at[i], r6.at[chip], dev)
        copy.start()
        sends.append(copy)
    exchange(chip).wait_recv()
    wr[chip] = wc[chip] + shares(chip, k)[...]

    for s, _ in others:
        remote(gx.at[s], gx.at[s], s5.at[0], r5.at[s], sibling).wait_recv()
    total = gx[0]
    for s in range(1, CHIPS):
        total = total + gx[s]
    gs[mine] = total
    copy = remote(gs.at[mine], gs.at[mine], s7, r7, sibling)
    copy.start()
    sends.append(copy)
    remote(gs.at[theirs], gs.at[theirs], s7, r7, sibling).wait_recv()
    ga = gs[0:64]
    gb = gs[64:96]
    upper = jnp.concatenate([gb, pltpu.roll(gb, 64, 1)], axis=0)
    top = jnp.where(lane64 < 64, ga, upper)
    low = top.T[64:]
    amat[0:64] = top
    amat[64:128] = jnp.where(lane64 < 64, jnp.concatenate([low, low], axis=1), ga)

    inverse_cholesky(amat)
    linv = amat[...]

    slot = chip * 2 + k
    for s, _ in others:
        remote(wr.at[s], wr.at[s], s6.at[0], r6.at[s], sibling).wait_recv()
    w = wr[0]
    for s in range(1, CHIPS):
        w = w + wr[s]
    f = lax.dot_general(w, linv, (((1,), (1,)), ((), ())), precision=HIGHEST, preferred_element_type=jnp.float32)
    sz[c] = jnp.broadcast_to(jnp.sum(f * f, axis=0, keepdims=True), (8, LANES))
    for o in far_first:
        t, dev = zpeer(o)
        copy = remote(sz.at[c], sz.at[c], s9.at[o], r9.at[c], dev)
        copy.start()
        sends.append(copy)
    fb[slot] = jnp.concatenate([f, jnp.zeros((fb.shape[1] - share, LANES), jnp.float32)], axis=0).astype(jnp.bfloat16)
    for i, (t, dev) in enumerate(others):
        copy = remote(fb.at[slot], fb.at[slot], s8.at[i], r8.at[slot], dev)
        copy.start()
        sends.append(copy)

    def forward(t):
        place = t * 2 + k
        return remote(fb.at[place], fb.at[place], sf.at[t], r8.at[place], sibling)

    forward(chip).start()
    ortho[...] = lax.dot_general(
        pw[...].reshape(rows, LANES), linv, (((1,), (1,)), ((), ())), precision=HIGHEST, preferred_element_type=jnp.float32
    ).astype(jnp.bfloat16)
    for o in (1, 7, 2, 6, 3, 5, 4):
        s = lax.rem(c + o, Z)
        remote(sz.at[s], sz.at[s], s9.at[0], r9.at[s], sibling).wait_recv()
    tot = sz[0]
    for s in range(1, Z):
        tot = tot + sz[s]
    sx[chip] = tot

    for i, (t, dev) in enumerate(others):
        copy = remote(sx.at[chip], sx.at[chip], s10.at[i], r10.at[chip], dev)
        copy.start()
        sends.append(copy)

    for t, _ in others:
        forward(t).wait_recv()
        forward(t).start()
    for s, _ in others:
        remote(sx.at[s], sx.at[s], s10.at[0], r10.at[s], sibling).wait_recv()
    tot = sx[0]
    for s in range(1, CHIPS):
        tot = tot + sx[s]
    sc[k] = tot
    copy = remote(sc.at[k], sc.at[k], s11, r11, sibling)
    copy.start()
    sends.append(copy)

    for t in range(CHIPS):
        place = t * 2 + other
        remote(fb.at[place], fb.at[place], sf.at[t], r8.at[place], sibling).wait_recv()
    for i in range(2 * CHIPS):
        factor[i * share : (i + 1) * share, :] = fb[i, 0:share].astype(jnp.float32)
    for t in range(tiles // 2):
        cols = slice(t * 2 * LANES, (t + 1) * 2 * LANES)
        d = lax.dot_general(
            ortho[...],
            factor[cols, :].astype(jnp.bfloat16),
            (((1,), (1,)), ((), ())),
            preferred_element_type=jnp.float32,
        )
        mnew[:, cols] = (buf[:, cols] - (1.0 - momentum_keep) * d).astype(jnp.bfloat16)

    remote(sc.at[other], sc.at[other], s11, r11, sibling).wait_recv()
    sq[...] = sc[0] + sc[1]

    for copy in sends:
        copy.wait_send()

    for t in range(CHIPS):
        exchange(t).wait_send()
        forward(t).wait_send()


def final_kernel(scaling, factor, ortho, sq, mnew, mout, direction, qnew, dbuf, qbuf, sem):
    copy = pltpu.make_async_copy(mnew, mout, sem.at[0, 0])
    copy.start()
    copies = [copy]
    inv = 1.0 / jnp.sqrt(sq[0:1] + epsilon)
    o = ortho[...]
    steps = factor.shape[0] // (2 * LANES)
    for part, (first, last) in enumerate(((0, 4), (4, 8), (8, steps))):
        for u in range(first, last):
            cols = slice(2 * u * LANES, 2 * (u + 1) * LANES)
            q = factor[cols, :] * inv
            qbuf[cols, :] = q
            update = lax.dot_general(
                o, q.astype(jnp.bfloat16), (((1,), (1,)), ((), ())), preferred_element_type=jnp.float32
            )
            dbuf[:, cols] = (scaling * update).astype(jnp.bfloat16)
        cols = pl.ds(first * 2 * LANES, (last - first) * 2 * LANES)
        for n, (src, dst) in enumerate(((dbuf.at[:, cols], direction.at[:, cols]), (qbuf.at[cols, :], qnew.at[cols, :]))):
            copy = pltpu.make_async_copy(src, dst, sem.at[1 + part, n])
            copy.start()
            copies.append(copy)
    for copy in copies:
        copy.wait()


def per_device(grad, momentum, q_prev):
    rows, cols = grad.shape
    share = cols // (2 * CHIPS)
    f32, bf16 = jnp.float32, jnp.bfloat16
    dma = pltpu.SemaphoreType.DMA
    vmem = pl.BlockSpec(memory_space=pltpu.VMEM)
    hbm = pl.BlockSpec(memory_space=pltpu.HBM)
    factor, ortho, sq, mnew = pl.pallas_call(
        main_kernel,
        out_shape=(
            jax.ShapeDtypeStruct((cols, LANES), f32),
            jax.ShapeDtypeStruct((rows, LANES), bf16),
            jax.ShapeDtypeStruct((8, LANES), f32),
            jax.ShapeDtypeStruct((rows, cols), bf16),
        ),
        in_specs=[hbm] * 3,
        out_specs=(vmem,) * 4,
        scratch_shapes=[
            pltpu.VMEM((rows, cols), bf16),
            pltpu.VMEM((rows, cols), bf16),
            pltpu.VMEM((cols, LANES), f32),
            pltpu.VMEM((rows, cols), f32),
            pltpu.VMEM((rows, cols), bf16),
            pltpu.VMEM((Z, rows // Z, LANES), f32),
            pltpu.VMEM((Z, rows // Z, LANES), f32),
            pltpu.VMEM((Z, rows // Z, LANES), f32),
            pltpu.VMEM((rows, 3 * LANES), bf16),
            pltpu.VMEM((96, LANES), f32),
            pltpu.VMEM((48, LANES), f32),
            pltpu.VMEM((CHIPS, 48, LANES), f32),
            pltpu.VMEM((96, LANES), f32),
            pltpu.VMEM((LANES, LANES), f32),
            pltpu.VMEM((cols, LANES), f32),
            pltpu.VMEM((CHIPS, share, LANES), f32),
            pltpu.VMEM((CHIPS, share, LANES), f32),
            pltpu.VMEM((2 * CHIPS, -(-share // 16) * 16, LANES), bf16),
            pltpu.VMEM((Z, 8, LANES), f32),
            pltpu.VMEM((CHIPS, 8, LANES), f32),
            pltpu.VMEM((2, 8, LANES), f32),
            dma((4, 3)),
            dma((Z,)), dma((Z,)),
            dma((Z,)), dma((Z,)),
            dma, dma,
            dma((CHIPS,)), dma((CHIPS,)),
            dma((CHIPS,)), dma((CHIPS,)),
            dma((CHIPS,)), dma((CHIPS,)),
            dma, dma,
            dma((CHIPS,)), dma((2 * CHIPS,)),
            dma((Z,)), dma((Z,)),
            dma((CHIPS,)),
            dma((CHIPS,)), dma((CHIPS,)),
            dma, dma,
        ],
        compiler_params=pltpu.CompilerParams(
            collective_id=0, has_side_effects=True, vmem_limit_bytes=40 * 2**20
        ),
        name="power_gram_factor",
    )(*(pltpu.with_memory_space_constraint(x, pltpu.HBM) for x in (grad, momentum, q_prev)))

    total_rows = rows * lax.axis_size("row")
    total_cols = cols * lax.axis_size("col")
    scaling = math.sqrt(total_rows * total_cols / q_prev.shape[1])
    return pl.pallas_call(
        functools.partial(final_kernel, scaling),
        out_shape=(
            jax.ShapeDtypeStruct((rows, cols), bf16),
            jax.ShapeDtypeStruct((rows, cols), bf16),
            jax.ShapeDtypeStruct((cols, LANES), f32),
        ),
        in_specs=[vmem] * 4,
        out_specs=(hbm,) * 3,
        scratch_shapes=[pltpu.VMEM((rows, cols), bf16), pltpu.VMEM((cols, LANES), f32), dma((4, 2))],
        compiler_params=pltpu.CompilerParams(vmem_limit_bytes=24 * 2**20),
        name="outputs",
    )(factor, ortho, sq, mnew)


def solution(mesh):
    return jax.shard_map(
        per_device,
        mesh=mesh,
        in_specs=(P("row", "col"), P("row", "col"), P("col", None)),
        out_specs=(P("row", "col"), P("row", "col"), P("col", None)),
        check_vma=False,
    )
```

```python
import functools
import math

import jax
import jax.numpy as jnp
from jax import lax
from jax.experimental import pallas as pl
from jax.experimental.pallas import tpu as pltpu
from jax.sharding import PartitionSpec as P

momentum_keep = 0.9
epsilon = 1e-06
MESH = pl.DeviceIdType.MESH
HIGHEST = lax.Precision.HIGHEST
LANES = 128
Z = 8
CHIPS = 16


def remote(src, dst, send, recv, device):
    return pltpu.make_async_remote_copy(
        src_ref=src, dst_ref=dst, send_sem=send, recv_sem=recv, device_id=device, device_id_type=MESH
    )


def inverse_cholesky(a_ref, out_ref):
    rank = a_ref.shape[0]
    size = 16
    lane = lax.broadcasted_iota(jnp.int32, (size, LANES), 1)
    sub = lax.broadcasted_iota(jnp.int32, (size, LANES), 0)

    def row(x, j):
        return jnp.broadcast_to(x[j : j + 1, :], (size, LANES))

    def blocks(first, last):
        low = first * size
        lane_all = lax.broadcasted_iota(jnp.int32, (rank - low, LANES), 1)

        def block(b, _):
            rows = pl.ds(pl.multiple_of(b * size, size), size)
            a = a_ref[low:rank, :]
            r = a_ref[rows, :]
            cols = [jnp.broadcast_to(r[:, k : k + 1], (size, LANES)) for k in range(size)]
            q = jnp.where(lane < size, 0.0, r)
            v = jnp.zeros((size, LANES), jnp.float32)
            pivots = jnp.zeros((size, LANES), jnp.float32)
            inverses = jnp.zeros((size, LANES), jnp.float32)
            for j in range(size):
                pivot = row(cols[j], j)
                inv = 1.0 / pivot
                here = sub == j
                m = jnp.where(here, 0.0, cols[j] * inv)
                qj = row(q, j) + jnp.where(lane == j, 1.0, 0.0)
                pivots = jnp.where(here, pivot, pivots)
                inverses = jnp.where(here, inv, inverses)
                v = jnp.where(here, qj, v)
                q = jnp.where(here, qj, q - m * qj)
                for k in range(j + 1, size):
                    cols[k] = cols[k] - m * row(cols[k], j)
            q = q * inverses
            total = jnp.zeros((rank - low, LANES), jnp.float32)
            for k in range(size):
                total = total + a[:, k : k + 1] * q[k : k + 1, :]
            a_ref[low:rank, :] = pltpu.roll(jnp.where(lane_all < size, 0.0, a) - total, LANES - size, 1)
            v = pltpu.roll(v * lax.rsqrt(pivots), b * size, 1)
            out_ref[rows, :] = jnp.where(lane < (b + 1) * size, v, 0.0)
            return 0

        lax.fori_loop(first, last, block, 0)

    quarter = rank // size // 4
    for i in range(4):
        blocks(i * quarter, (i + 1) * quarter)


FAR = [(dy, dx) for dy in (2, 1, 3, 0) for dx in (2, 1, 3, 0) if (dy, dx) != (0, 0)]
NEAR = sorted(FAR, key=lambda d: min(d[0], 4 - d[0]) + min(d[1], 4 - d[1]))
W_ORDER, G_ORDER, F_ORDER, S_ORDER = NEAR, FAR, FAR, FAR


def main_kernel(
    grad, mom, qprev, factor, ortho, sq, mnew,
    gbuf, mbuf, qbuf, buf, bb, pp, prs, pw, pt, p2, gh, cg, gx, gs, amat, lmat, wt, wc, wr, fb, sz, sx,
    in_sem, s1, r1, s2, r2, s3, r3, s4, r4, s5, r5, s6, r6, s7, r7, s8, r8, s9, r9, sf, s10, r10,
):
    rowi = lax.axis_index("row")
    c = lax.axis_index("col")
    chip = rowi // 2
    k = lax.rem(rowi, 2)
    other = 1 - k
    sibling = (chip * 2 + other, c)
    tiles = bb.shape[1] // LANES
    share = wr.shape[1]

    def zpeer(o):
        t = lax.rem(c + o, Z)
        return t, (rowi, t)

    def zother(o):
        return (chip * 2 + other, lax.rem(c + o, Z))

    def cpeer(d):
        t = lax.rem(chip // 4 + d[0], 4) * 4 + lax.rem(chip + d[1], 4)
        return t, (t * 2 + k, c)

    others = [cpeer(d) for d in NEAR]
    w_others = [cpeer(d) for d in W_ORDER]
    g_others = [cpeer(d) for d in G_ORDER]
    f_others = [cpeer(d) for d in F_ORDER]
    s_others = [cpeer(d) for d in S_ORDER]

    far_first = (4, 3, 5, 2, 6, 1, 7)
    barrier = pltpu.get_barrier_semaphore()

    for o in far_first:
        pl.semaphore_signal(barrier, inc=1, device_id=zpeer(o)[1], device_id_type=MESH)
    for o in far_first:
        pl.semaphore_signal(barrier, inc=1, device_id=zother(o), device_id_type=MESH)
    for _, dev in others:
        pl.semaphore_signal(barrier, inc=1, device_id=dev, device_id_type=MESH)
    pl.semaphore_signal(barrier, inc=1, device_id=sibling, device_id_type=MESH)

    bounds = [0, 7, 14, 20, tiles]
    loads = []
    for i in range(4):
        lanes = pl.ds(bounds[i] * LANES, (bounds[i + 1] - bounds[i]) * LANES)
        part = [
            pltpu.make_async_copy(grad.at[:, lanes], gbuf.at[:, lanes], in_sem.at[i, 0]),
            pltpu.make_async_copy(mom.at[:, lanes], mbuf.at[:, lanes], in_sem.at[i, 1]),
            pltpu.make_async_copy(qprev.at[lanes, :], qbuf.at[lanes, :], in_sem.at[i, 2]),
        ]
        for copy in part:
            copy.start()
        loads.append(part)

    rows = bb.shape[0]
    for i in range(4):
        for copy in loads[i]:
            copy.wait()
        lanes = pl.ds(bounds[i] * LANES, (bounds[i + 1] - bounds[i]) * LANES)

        def strip(s, _):
            rs = pl.ds(pl.multiple_of(s * 32, 32), 32)
            g = gbuf[rs, lanes].astype(jnp.float32)
            m = mbuf[rs, lanes].astype(jnp.float32)
            b = momentum_keep * m + g
            buf[rs, lanes] = b
            bb[rs, lanes] = b.astype(jnp.bfloat16)
            return 0

        lax.fori_loop(0, rows // 32, strip, 0)
        d = jnp.dot(bb[:, lanes], qbuf[lanes, :].astype(jnp.bfloat16), preferred_element_type=jnp.float32)
        d = d.reshape(Z, rows // Z, LANES)
        pp[...] = d if i == 0 else pp[...] + d

    pl.semaphore_wait(barrier, 2 * (Z - 1) + CHIPS - 1 + 1)

    sends = []
    for o in far_first:
        t, dev = zpeer(o)
        copy = remote(pp.at[t], prs.at[c], s1.at[o], r1.at[c], dev)
        copy.start()
        sends.append(copy)
    red = pp[c]
    for o in (1, 7, 2, 6, 3, 5, 4):
        s = lax.rem(c + o, Z)
        remote(pp.at[s], prs.at[s], s1.at[0], r1.at[s], sibling).wait_recv()
        red = red + prs[s]
    pw[c] = red
    for o in far_first:
        t, dev = zpeer(o)
        copy = remote(pw.at[c], pw.at[c], s2.at[o], r2.at[c], dev)
        copy.start()
        sends.append(copy)
    for o in (1, 7, 2, 6, 3, 5, 4):
        s = lax.rem(c + o, Z)
        remote(pw.at[s], pw.at[s], s2.at[0], r2.at[s], sibling).wait_recv()

    power = pw[...].reshape(rows, LANES)
    hi = power.astype(jnp.bfloat16)
    p2[:, 0:128] = hi
    p2[:, 128:256] = (power - hi.astype(jnp.float32)).astype(jnp.bfloat16)
    for i in range(4):
        start, stop = bounds[i] * LANES, bounds[i + 1] * LANES
        d = lax.dot_general(
            bb[:, start:stop], p2[...], (((0,), (0,)), ((), ())), preferred_element_type=jnp.float32
        )
        d = d[:, 0:128] + d[:, 128:256]
        for place in range(start // share, -(-stop // share)):
            a, b = max(start, place * share), min(stop, (place + 1) * share)
            wt[place // 2, place % 2, a - place * share : b - place * share, :] = d[a - start : b - start]

    def exchange(u):
        return remote(wt.at[u, other], wc.at[u], s4.at[u], r4.at[u], sibling)

    for u, _ in w_others:
        exchange(u).start()
    exchange(chip).start()

    pt[...] = power.T
    part = pt[pl.ds(pl.multiple_of(c * 16, 16), 16), :]
    part = jnp.dot(part, power, precision=HIGHEST, preferred_element_type=jnp.float32)
    gh[...] = part.reshape(2, 8, LANES)
    copy = remote(gh.at[other], cg, s3, r3, sibling)
    copy.start()
    sends.append(copy)

    remote(cg, cg, s3, r3, sibling).wait_recv()
    gx[chip] = gh[k] + cg[...]
    for i, (t, dev) in enumerate(g_others):
        copy = remote(gx.at[chip], gx.at[chip], s5.at[i], r5.at[chip], dev)
        copy.start()
        sends.append(copy)

    for i, (u, dev) in enumerate(w_others):
        exchange(u).wait_recv()
        wc[u] = wc[u] + wt[u, k]
        copy = remote(wc.at[u], wr.at[chip], s6.at[i], r6.at[chip], dev)
        copy.start()
        sends.append(copy)
    exchange(chip).wait_recv()
    wr[chip] = wc[chip] + wt[chip, k]

    for s, _ in others:
        remote(gx.at[s], gx.at[s], s5.at[0], r5.at[s], sibling).wait_recv()
    total = gx[0]
    for s in range(1, CHIPS):
        total = total + gx[s]
    eight = 2 * c + k

    def spread(ref, send, recv):
        for o in far_first:
            for core, dev in enumerate((zpeer(o)[1], zother(o))):
                copy = remote(ref.at[eight], ref.at[eight], send.at[core, o], recv.at[eight], dev)
                copy.start()
                sends.append(copy)
        copy = remote(ref.at[eight], ref.at[eight], send.at[0, 0], recv.at[eight], sibling)
        copy.start()
        sends.append(copy)

    def collect(ref, send, recv):
        for o in (0, 1, 7, 2, 6, 3, 5, 4):
            for core in (other,) if o == 0 else (k, other):
                s = 2 * lax.rem(c + o, Z) + core
                remote(ref.at[s], ref.at[s], send.at[0, 0], recv.at[s], sibling).wait_recv()

    gs[eight] = total
    spread(gs, s7, r7)
    collect(gs, s7, r7)
    amat[...] = gs[...].reshape(LANES, LANES)

    inverse_cholesky(amat, lmat)
    linv = lmat[...]

    slot = chip * 2 + k
    for s, _ in others:
        remote(wr.at[s], wr.at[s], s6.at[0], r6.at[s], sibling).wait_recv()
    w = wr[0]
    for s in range(1, CHIPS):
        w = w + wr[s]
    f = lax.dot_general(w, linv, (((1,), (1,)), ((), ())), precision=HIGHEST, preferred_element_type=jnp.float32)
    sz[eight] = jnp.broadcast_to(jnp.sum(f * f, axis=0, keepdims=True), (8, LANES))
    spread(sz, s9, r9)
    fb[slot] = jnp.concatenate([f, jnp.zeros((fb.shape[1] - share, LANES), jnp.float32)], axis=0).astype(jnp.bfloat16)
    for i, (t, dev) in enumerate(f_others):
        copy = remote(fb.at[slot], fb.at[slot], s8.at[i], r8.at[slot], dev)
        copy.start()
        sends.append(copy)

    def forward(t):
        place = t * 2 + k
        return remote(fb.at[place], fb.at[place], sf.at[t], r8.at[place], sibling)

    forward(chip).start()
    ortho[...] = lax.dot_general(
        pw[...].reshape(rows, LANES), linv, (((1,), (1,)), ((), ())), precision=HIGHEST, preferred_element_type=jnp.float32
    ).astype(jnp.bfloat16)
    collect(sz, s9, r9)
    tot = sz[0]
    for s in range(1, 2 * Z):
        tot = tot + sz[s]
    sx[chip] = tot

    for i, (t, dev) in enumerate(s_others):
        copy = remote(sx.at[chip], sx.at[chip], s10.at[i], r10.at[chip], dev)
        copy.start()
        sends.append(copy)

    for t, _ in f_others:
        forward(t).wait_recv()
        forward(t).start()
    for s, _ in others:
        remote(sx.at[s], sx.at[s], s10.at[0], r10.at[s], sibling).wait_recv()
    tot = sx[0]
    for s in range(1, CHIPS):
        tot = tot + sx[s]
    sq[...] = tot

    for t in range(CHIPS):
        place = t * 2 + other
        remote(fb.at[place], fb.at[place], sf.at[t], r8.at[place], sibling).wait_recv()
    for i in range(2 * CHIPS):
        factor[i * share : (i + 1) * share, :] = fb[i, 0:share].astype(jnp.float32)
    for t in range(tiles // 2):
        cols = slice(t * 2 * LANES, (t + 1) * 2 * LANES)
        d = lax.dot_general(
            ortho[...],
            factor[cols, :].astype(jnp.bfloat16),
            (((1,), (1,)), ((), ())),
            preferred_element_type=jnp.float32,
        )
        mnew[:, cols] = (buf[:, cols] - (1.0 - momentum_keep) * d).astype(jnp.bfloat16)

    for copy in sends:
        copy.wait_send()

    for t in range(CHIPS):
        exchange(t).wait_send()
        forward(t).wait_send()


def final_kernel(scaling, factor, ortho, sq, mnew, mout, direction, qnew, dbuf, qbuf, sem):
    copy = pltpu.make_async_copy(mnew, mout, sem.at[0, 0])
    copy.start()
    copies = [copy]
    inv = 1.0 / jnp.sqrt(sq[0:1] + epsilon)
    o = ortho[...]
    steps = factor.shape[0] // (2 * LANES)
    for part, (first, last) in enumerate(((0, 4), (4, 8), (8, steps))):
        for u in range(first, last):
            cols = slice(2 * u * LANES, 2 * (u + 1) * LANES)
            q = factor[cols, :] * inv
            qbuf[cols, :] = q
            update = lax.dot_general(
                o, q.astype(jnp.bfloat16), (((1,), (1,)), ((), ())), preferred_element_type=jnp.float32
            )
            dbuf[:, cols] = (scaling * update).astype(jnp.bfloat16)
        cols = pl.ds(first * 2 * LANES, (last - first) * 2 * LANES)
        for n, (src, dst) in enumerate(((dbuf.at[:, cols], direction.at[:, cols]), (qbuf.at[cols, :], qnew.at[cols, :]))):
            copy = pltpu.make_async_copy(src, dst, sem.at[1 + part, n])
            copy.start()
            copies.append(copy)
    for copy in copies:
        copy.wait()


def per_device(grad, momentum, q_prev):
    rows, cols = grad.shape
    share = cols // (2 * CHIPS)
    f32, bf16 = jnp.float32, jnp.bfloat16
    dma = pltpu.SemaphoreType.DMA
    vmem = pl.BlockSpec(memory_space=pltpu.VMEM)
    hbm = pl.BlockSpec(memory_space=pltpu.HBM)
    factor, ortho, sq, mnew = pl.pallas_call(
        main_kernel,
        out_shape=(
            jax.ShapeDtypeStruct((cols, LANES), f32),
            jax.ShapeDtypeStruct((rows, LANES), bf16),
            jax.ShapeDtypeStruct((8, LANES), f32),
            jax.ShapeDtypeStruct((rows, cols), bf16),
        ),
        in_specs=[hbm] * 3,
        out_specs=(vmem,) * 4,
        scratch_shapes=[
            pltpu.VMEM((rows, cols), bf16),
            pltpu.VMEM((rows, cols), bf16),
            pltpu.VMEM((cols, LANES), f32),
            pltpu.VMEM((rows, cols), f32),
            pltpu.VMEM((rows, cols), bf16),
            pltpu.VMEM((Z, rows // Z, LANES), f32),
            pltpu.VMEM((Z, rows // Z, LANES), f32),
            pltpu.VMEM((Z, rows // Z, LANES), f32),
            pltpu.VMEM((LANES, rows), f32),
            pltpu.VMEM((rows, 2 * LANES), bf16),
            pltpu.VMEM((2, 8, LANES), f32),
            pltpu.VMEM((8, LANES), f32),
            pltpu.VMEM((CHIPS, 8, LANES), f32),
            pltpu.VMEM((2 * Z, 8, LANES), f32),
            pltpu.VMEM((LANES, LANES), f32),
            pltpu.VMEM((LANES, LANES), f32),
            pltpu.VMEM((CHIPS, 2, share, LANES), f32),
            pltpu.VMEM((CHIPS, share, LANES), f32),
            pltpu.VMEM((CHIPS, share, LANES), f32),
            pltpu.VMEM((2 * CHIPS, -(-share // 16) * 16, LANES), bf16),
            pltpu.VMEM((2 * Z, 8, LANES), f32),
            pltpu.VMEM((CHIPS, 8, LANES), f32),
            dma((4, 3)),
            dma((Z,)), dma((Z,)),
            dma((Z,)), dma((Z,)),
            dma, dma,
            dma((CHIPS,)), dma((CHIPS,)),
            dma((CHIPS,)), dma((CHIPS,)),
            dma((CHIPS,)), dma((CHIPS,)),
            dma((2, Z)), dma((2 * Z,)),
            dma((CHIPS,)), dma((2 * CHIPS,)),
            dma((2, Z)), dma((2 * Z,)),
            dma((CHIPS,)),
            dma((CHIPS,)), dma((CHIPS,)),
        ],
        compiler_params=pltpu.CompilerParams(
            collective_id=0, has_side_effects=True, vmem_limit_bytes=40 * 2**20
        ),
        name="power_gram_factor",
    )(*(pltpu.with_memory_space_constraint(x, pltpu.HBM) for x in (grad, momentum, q_prev)))

    total_rows = rows * lax.axis_size("row")
    total_cols = cols * lax.axis_size("col")
    scaling = math.sqrt(total_rows * total_cols / q_prev.shape[1])
    return pl.pallas_call(
        functools.partial(final_kernel, scaling),
        out_shape=(
            jax.ShapeDtypeStruct((rows, cols), bf16),
            jax.ShapeDtypeStruct((rows, cols), bf16),
            jax.ShapeDtypeStruct((cols, LANES), f32),
        ),
        in_specs=[vmem] * 4,
        out_specs=(hbm,) * 3,
        scratch_shapes=[pltpu.VMEM((rows, cols), bf16), pltpu.VMEM((cols, LANES), f32), dma((4, 2))],
        compiler_params=pltpu.CompilerParams(vmem_limit_bytes=24 * 2**20),
        name="outputs",
    )(factor, ortho, sq, mnew)


def solution(mesh):
    return jax.shard_map(
        per_device,
        mesh=mesh,
        in_specs=(P("row", "col"), P("row", "col"), P("col", None)),
        out_specs=(P("row", "col"), P("row", "col"), P("col", None)),
        check_vma=False,
    )
```

```python
import functools
import math

import jax
import jax.numpy as jnp
from jax import lax
from jax.experimental import pallas as pl
from jax.experimental.pallas import tpu as pltpu
from jax.sharding import PartitionSpec as P

momentum_keep = 0.9
epsilon = 1e-06
MESH = pl.DeviceIdType.MESH
HIGHEST = lax.Precision.HIGHEST
LANES = 128
Z = 8
CHIPS = 16


def remote(src, dst, send, recv, device):
    return pltpu.make_async_remote_copy(
        src_ref=src, dst_ref=dst, send_sem=send, recv_sem=recv, device_id=device, device_id_type=MESH
    )


def inverse_cholesky(a_ref, out_ref):
    rank = a_ref.shape[0]
    size = 16
    lane = lax.broadcasted_iota(jnp.int32, (size, LANES), 1)
    sub = lax.broadcasted_iota(jnp.int32, (size, LANES), 0)

    def row(x, j):
        return jnp.broadcast_to(x[j : j + 1, :], (size, LANES))

    def blocks(first, last):
        low = first * size
        lane_all = lax.broadcasted_iota(jnp.int32, (rank - low, LANES), 1)

        def block(b, _):
            rows = pl.ds(pl.multiple_of(b * size, size), size)
            a = a_ref[low:rank, :]
            r = a_ref[rows, :]
            cols = [jnp.broadcast_to(r[:, k : k + 1], (size, LANES)) for k in range(size)]
            q = jnp.where(lane < size, 0.0, r)
            v = jnp.zeros((size, LANES), jnp.float32)
            pivots = jnp.zeros((size, LANES), jnp.float32)
            inverses = jnp.zeros((size, LANES), jnp.float32)
            for j in range(size):
                pivot = row(cols[j], j)
                inv = 1.0 / pivot
                here = sub == j
                m = jnp.where(here, 0.0, cols[j] * inv)
                qj = row(q, j) + jnp.where(lane == j, 1.0, 0.0)
                pivots = jnp.where(here, pivot, pivots)
                inverses = jnp.where(here, inv, inverses)
                v = jnp.where(here, qj, v)
                q = jnp.where(here, qj, q - m * qj)
                for k in range(j + 1, size):
                    cols[k] = cols[k] - m * row(cols[k], j)
            q = q * inverses
            total = jnp.zeros((rank - low, LANES), jnp.float32)
            for k in range(size):
                total = total + a[:, k : k + 1] * q[k : k + 1, :]
            a_ref[low:rank, :] = pltpu.roll(jnp.where(lane_all < size, 0.0, a) - total, LANES - size, 1)
            v = pltpu.roll(v * lax.rsqrt(pivots), b * size, 1)
            out_ref[rows, :] = jnp.where(lane < (b + 1) * size, v, 0.0)
            return 0

        lax.fori_loop(first, last, block, 0)

    quarter = rank // size // 4
    for i in range(4):
        blocks(i * quarter, (i + 1) * quarter)


FAR = [(dy, dx) for dy in (2, 1, 3, 0) for dx in (2, 1, 3, 0) if (dy, dx) != (0, 0)]
NEAR = sorted(FAR, key=lambda d: min(d[0], 4 - d[0]) + min(d[1], 4 - d[1]))
W_ORDER, G_ORDER, F_ORDER, S_ORDER = NEAR, FAR, FAR, FAR


def main_kernel(
    grad, mom, qprev, factor, ortho, sq, buf,
    gbuf, mbuf, qbuf, bb, pp, prs, pw, pt, p2, gh, cg, gx, gs, amat, lmat, wt, wc, wr, fb, sz, sx,
    in_sem, s1, r1, s2, r2, s3, r3, s4, r4, s5, r5, s6, r6, s7, r7, s8, r8, s9, r9, sf, s10, r10,
):
    rowi = lax.axis_index("row")
    c = lax.axis_index("col")
    chip = rowi // 2
    k = lax.rem(rowi, 2)
    other = 1 - k
    sibling = (chip * 2 + other, c)
    tiles = bb.shape[1] // LANES
    share = wr.shape[1]

    def zpeer(o):
        t = lax.rem(c + o, Z)
        return t, (rowi, t)

    def zother(o):
        return (chip * 2 + other, lax.rem(c + o, Z))

    def cpeer(d):
        t = lax.rem(chip // 4 + d[0], 4) * 4 + lax.rem(chip + d[1], 4)
        return t, (t * 2 + k, c)

    others = [cpeer(d) for d in NEAR]
    w_others = [cpeer(d) for d in W_ORDER]
    g_others = [cpeer(d) for d in G_ORDER]
    f_others = [cpeer(d) for d in F_ORDER]
    s_others = [cpeer(d) for d in S_ORDER]

    far_first = (4, 3, 5, 2, 6, 1, 7)
    barrier = pltpu.get_barrier_semaphore()

    for o in far_first:
        pl.semaphore_signal(barrier, inc=1, device_id=zpeer(o)[1], device_id_type=MESH)
    for o in far_first:
        pl.semaphore_signal(barrier, inc=1, device_id=zother(o), device_id_type=MESH)
    for _, dev in others:
        pl.semaphore_signal(barrier, inc=1, device_id=dev, device_id_type=MESH)
    pl.semaphore_signal(barrier, inc=1, device_id=sibling, device_id_type=MESH)

    bounds = [0, 8, 15, 21, tiles - 2, tiles]
    loads = []
    for i in range(5):
        lanes = pl.ds(bounds[i] * LANES, (bounds[i + 1] - bounds[i]) * LANES)
        part = [
            pltpu.make_async_copy(grad.at[:, lanes], gbuf.at[:, lanes], in_sem.at[i, 0]),
            pltpu.make_async_copy(mom.at[:, lanes], mbuf.at[:, lanes], in_sem.at[i, 1]),
            pltpu.make_async_copy(qprev.at[lanes, :], qbuf.at[lanes, :], in_sem.at[i, 2]),
        ]
        for copy in part:
            copy.start()
        loads.append(part)

    rows = bb.shape[0]
    for i in range(5):
        for copy in loads[i]:
            copy.wait()
        lanes = pl.ds(bounds[i] * LANES, (bounds[i + 1] - bounds[i]) * LANES)

        def strip(s, _):
            rs = pl.ds(pl.multiple_of(s * 32, 32), 32)
            g = gbuf[rs, lanes].astype(jnp.float32)
            m = mbuf[rs, lanes].astype(jnp.float32)
            b = momentum_keep * m + g
            buf[rs, lanes] = b
            bb[rs, lanes] = b.astype(jnp.bfloat16)
            return 0

        lax.fori_loop(0, rows // 32, strip, 0)
        d = jnp.dot(bb[:, lanes], qbuf[lanes, :].astype(jnp.bfloat16), preferred_element_type=jnp.float32)
        d = d.reshape(Z, rows // Z, LANES)
        pp[...] = d if i == 0 else pp[...] + d

    pl.semaphore_wait(barrier, 2 * (Z - 1) + CHIPS - 1 + 1)

    sends, late = [], []

    def drain(copies):
        for copy in copies:
            copy.wait_send()
        copies.clear()

    for o in far_first:
        t, dev = zpeer(o)
        copy = remote(pp.at[t], prs.at[c], s1.at[o], r1.at[c], dev)
        copy.start()
        sends.append(copy)
    red = pp[c]
    for o in (1, 7, 2, 6, 3, 5, 4):
        s = lax.rem(c + o, Z)
        remote(pp.at[s], prs.at[s], s1.at[0], r1.at[s], sibling).wait_recv()
        red = red + prs[s]
    pw[c] = red
    for o in far_first:
        t, dev = zpeer(o)
        copy = remote(pw.at[c], pw.at[c], s2.at[o], r2.at[c], dev)
        copy.start()
        sends.append(copy)
    for o in (1, 7, 2, 6, 3, 5, 4):
        s = lax.rem(c + o, Z)
        remote(pw.at[s], pw.at[s], s2.at[0], r2.at[s], sibling).wait_recv()

    power = pw[...].reshape(rows, LANES)
    hi = power.astype(jnp.bfloat16)
    p2[:, 0:128] = hi
    p2[:, 128:256] = (power - hi.astype(jnp.float32)).astype(jnp.bfloat16)
    for i in range(5):
        start, stop = bounds[i] * LANES, bounds[i + 1] * LANES
        d = lax.dot_general(
            bb[:, start:stop], p2[...], (((0,), (0,)), ((), ())), preferred_element_type=jnp.float32
        )
        d = d[:, 0:128] + d[:, 128:256]
        for place in range(start // share, -(-stop // share)):
            a, b = max(start, place * share), min(stop, (place + 1) * share)
            wt[place // 2, place % 2, a - place * share : b - place * share, :] = d[a - start : b - start]

    def exchange(u):
        return remote(wt.at[u, other], wc.at[u], s4.at[u], r4.at[u], sibling)

    for u, _ in w_others:
        exchange(u).start()
    exchange(chip).start()

    pt[...] = power.T
    part = pt[pl.ds(pl.multiple_of(c * 16, 16), 16), :]
    part = jnp.dot(part, power, precision=HIGHEST, preferred_element_type=jnp.float32)
    gh[...] = part.reshape(2, 8, LANES)
    copy = remote(gh.at[other], cg, s3, r3, sibling)
    copy.start()
    sends.append(copy)

    remote(cg, cg, s3, r3, sibling).wait_recv()
    gx[chip] = gh[k] + cg[...]
    for i, (t, dev) in enumerate(g_others):
        copy = remote(gx.at[chip], gx.at[chip], s5.at[i], r5.at[chip], dev)
        copy.start()
        sends.append(copy)

    for i, (u, dev) in enumerate(w_others):
        exchange(u).wait_recv()
        wc[u] = wc[u] + wt[u, k]
        copy = remote(wc.at[u], wr.at[chip], s6.at[i], r6.at[chip], dev)
        copy.start()
        late.append(copy)
    exchange(chip).wait_recv()
    wr[chip] = wc[chip] + wt[chip, k]

    for s, _ in others:
        remote(gx.at[s], gx.at[s], s5.at[0], r5.at[s], sibling).wait_recv()
    total = gx[0]
    for s in range(1, CHIPS):
        total = total + gx[s]
    eight = 2 * c + k

    def spread(ref, send, recv, sends):
        for o in far_first:
            for core, dev in enumerate((zpeer(o)[1], zother(o))):
                copy = remote(ref.at[eight], ref.at[eight], send.at[core, o], recv.at[eight], dev)
                copy.start()
                sends.append(copy)
        copy = remote(ref.at[eight], ref.at[eight], send.at[0, 0], recv.at[eight], sibling)
        copy.start()
        sends.append(copy)

    def collect(ref, send, recv):
        for o in (0, 1, 7, 2, 6, 3, 5, 4):
            for core in (other,) if o == 0 else (k, other):
                s = 2 * lax.rem(c + o, Z) + core
                remote(ref.at[s], ref.at[s], send.at[0, 0], recv.at[s], sibling).wait_recv()

    gs[eight] = total
    early = sends
    sends = late
    spread(gs, s7, r7, sends)
    drain(early)
    for t in range(CHIPS):
        exchange(t).wait_send()
    collect(gs, s7, r7)
    amat[...] = gs[...].reshape(LANES, LANES)

    inverse_cholesky(amat, lmat)
    linv = lmat[...]

    slot = chip * 2 + k
    for s, _ in others:
        remote(wr.at[s], wr.at[s], s6.at[0], r6.at[s], sibling).wait_recv()
    w = wr[0]
    for s in range(1, CHIPS):
        w = w + wr[s]
    f = lax.dot_general(w, linv, (((1,), (1,)), ((), ())), precision=HIGHEST, preferred_element_type=jnp.float32)
    sz[eight] = jnp.broadcast_to(jnp.sum(f * f, axis=0, keepdims=True), (8, LANES))
    early, sends = sends, []
    spread(sz, s9, r9, sends)
    fb[slot] = jnp.concatenate([f, jnp.zeros((fb.shape[1] - share, LANES), jnp.float32)], axis=0).astype(jnp.bfloat16)
    shared = []
    for i, (t, dev) in enumerate(f_others):
        copy = remote(fb.at[slot], fb.at[slot], s8.at[i], r8.at[slot], dev)
        copy.start()
        shared.append(copy)

    def forward(t):
        place = t * 2 + k
        return remote(fb.at[place], fb.at[place], sf.at[t], r8.at[place], sibling)

    forward(chip).start()
    ortho[...] = lax.dot_general(
        pw[...].reshape(rows, LANES), linv, (((1,), (1,)), ((), ())), precision=HIGHEST, preferred_element_type=jnp.float32
    ).astype(jnp.bfloat16)
    drain(early)
    collect(sz, s9, r9)
    tot = sz[0]
    for s in range(1, 2 * Z):
        tot = tot + sz[s]
    sx[chip] = tot

    last = []
    for i, (t, dev) in enumerate(s_others):
        copy = remote(sx.at[chip], sx.at[chip], s10.at[i], r10.at[chip], dev)
        copy.start()
        last.append(copy)

    drain(sends)
    for t, _ in f_others:
        forward(t).wait_recv()
        forward(t).start()
    drain(shared)
    for s, _ in others:
        remote(sx.at[s], sx.at[s], s10.at[0], r10.at[s], sibling).wait_recv()
    tot = sx[0]
    for s in range(1, CHIPS):
        tot = tot + sx[s]
    sq[...] = tot

    for t in range(CHIPS):
        place = t * 2 + other
        remote(fb.at[place], fb.at[place], sf.at[t], r8.at[place], sibling).wait_recv()
    for i in range(2 * CHIPS):
        factor[i * share : (i + 1) * share, :] = fb[i, 0:share].astype(jnp.float32)
    drain(last)
    for t in range(CHIPS):
        forward(t).wait_send()


def final_kernel(scaling, factor, ortho, sq, buf, mout, direction, qnew, mbuf, dbuf, qbuf, sem):
    inv = 1.0 / jnp.sqrt(sq[0:1] + epsilon)
    o = ortho[...]
    steps = factor.shape[0] // (2 * LANES)
    copies = []

    def times(x):
        return lax.dot_general(
            o, x.astype(jnp.bfloat16), (((1,), (1,)), ((), ())), preferred_element_type=jnp.float32
        )

    for part, (first, last) in enumerate(((0, 3), (3, 8), (8, steps))):
        cols = slice(first * 2 * LANES, last * 2 * LANES)
        for u in range(first, last):
            c = slice(2 * u * LANES, 2 * (u + 1) * LANES)
            q = factor[c, :] * inv
            qbuf[c, :] = q
            dbuf[:, c] = (scaling * times(q)).astype(jnp.bfloat16)
            mbuf[:, c] = (buf[:, c] - (1.0 - momentum_keep) * times(factor[c, :])).astype(jnp.bfloat16)
        pairs = (
            (qbuf.at[cols, :], qnew.at[cols, :]),
            (dbuf.at[:, cols], direction.at[:, cols]),
            (mbuf.at[:, cols], mout.at[:, cols]),
        )
        for n, (src, dst) in enumerate(pairs):
            copy = pltpu.make_async_copy(src, dst, sem.at[part, n])
            copy.start()
            copies.append(copy)
    for copy in copies:
        copy.wait()


def per_device(grad, momentum, q_prev):
    rows, cols = grad.shape
    share = cols // (2 * CHIPS)
    f32, bf16 = jnp.float32, jnp.bfloat16
    dma = pltpu.SemaphoreType.DMA
    vmem = pl.BlockSpec(memory_space=pltpu.VMEM)
    hbm = pl.BlockSpec(memory_space=pltpu.HBM)
    factor, ortho, sq, buffer = pl.pallas_call(
        main_kernel,
        out_shape=(
            jax.ShapeDtypeStruct((cols, LANES), f32),
            jax.ShapeDtypeStruct((rows, LANES), bf16),
            jax.ShapeDtypeStruct((8, LANES), f32),
            jax.ShapeDtypeStruct((rows, cols), f32),
        ),
        in_specs=[hbm] * 3,
        out_specs=(vmem,) * 4,
        scratch_shapes=[
            pltpu.VMEM((rows, cols), bf16),
            pltpu.VMEM((rows, cols), bf16),
            pltpu.VMEM((cols, LANES), f32),
            pltpu.VMEM((rows, cols), bf16),
            pltpu.VMEM((Z, rows // Z, LANES), f32),
            pltpu.VMEM((Z, rows // Z, LANES), f32),
            pltpu.VMEM((Z, rows // Z, LANES), f32),
            pltpu.VMEM((LANES, rows), f32),
            pltpu.VMEM((rows, 2 * LANES), bf16),
            pltpu.VMEM((2, 8, LANES), f32),
            pltpu.VMEM((8, LANES), f32),
            pltpu.VMEM((CHIPS, 8, LANES), f32),
            pltpu.VMEM((2 * Z, 8, LANES), f32),
            pltpu.VMEM((LANES, LANES), f32),
            pltpu.VMEM((LANES, LANES), f32),
            pltpu.VMEM((CHIPS, 2, share, LANES), f32),
            pltpu.VMEM((CHIPS, share, LANES), f32),
            pltpu.VMEM((CHIPS, share, LANES), f32),
            pltpu.VMEM((2 * CHIPS, -(-share // 16) * 16, LANES), bf16),
            pltpu.VMEM((2 * Z, 8, LANES), f32),
            pltpu.VMEM((CHIPS, 8, LANES), f32),
            dma((5, 3)),
            dma((Z,)), dma((Z,)),
            dma((Z,)), dma((Z,)),
            dma, dma,
            dma((CHIPS,)), dma((CHIPS,)),
            dma((CHIPS,)), dma((CHIPS,)),
            dma((CHIPS,)), dma((CHIPS,)),
            dma((2, Z)), dma((2 * Z,)),
            dma((CHIPS,)), dma((2 * CHIPS,)),
            dma((2, Z)), dma((2 * Z,)),
            dma((CHIPS,)),
            dma((CHIPS,)), dma((CHIPS,)),
        ],
        compiler_params=pltpu.CompilerParams(
            collective_id=0, has_side_effects=True, vmem_limit_bytes=40 * 2**20
        ),
        name="power_gram_factor",
    )(*(pltpu.with_memory_space_constraint(x, pltpu.HBM) for x in (grad, momentum, q_prev)))

    total_rows = rows * lax.axis_size("row")
    total_cols = cols * lax.axis_size("col")
    scaling = math.sqrt(total_rows * total_cols / q_prev.shape[1])
    return pl.pallas_call(
        functools.partial(final_kernel, scaling),
        out_shape=(
            jax.ShapeDtypeStruct((rows, cols), bf16),
            jax.ShapeDtypeStruct((rows, cols), bf16),
            jax.ShapeDtypeStruct((cols, LANES), f32),
        ),
        in_specs=[vmem] * 4,
        out_specs=(hbm,) * 3,
        scratch_shapes=[
            pltpu.VMEM((rows, cols), bf16),
            pltpu.VMEM((rows, cols), bf16),
            pltpu.VMEM((cols, LANES), f32),
            dma((3, 3)),
        ],
        compiler_params=pltpu.CompilerParams(vmem_limit_bytes=24 * 2**20),
        name="outputs",
    )(factor, ortho, sq, buffer)


def solution(mesh):
    return jax.shard_map(
        per_device,
        mesh=mesh,
        in_specs=(P("row", "col"), P("row", "col"), P("col", None)),
        out_specs=(P("row", "col"), P("row", "col"), P("col", None)),
        check_vma=False,
    )
```

```python
import functools
import math

import jax
import jax.numpy as jnp
from jax import lax
from jax.experimental import pallas as pl
from jax.experimental.pallas import tpu as pltpu
from jax.sharding import PartitionSpec as P

momentum_keep = 0.9
epsilon = 1e-06
MESH = pl.DeviceIdType.MESH
HIGHEST = lax.Precision.HIGHEST
LANES = 128
Z = 8
CHIPS = 16


def remote(src, dst, send, recv, device):
    return pltpu.make_async_remote_copy(
        src_ref=src, dst_ref=dst, send_sem=send, recv_sem=recv, device_id=device, device_id_type=MESH
    )


def inverse_cholesky(a_ref, out_ref):
    rank = a_ref.shape[0]
    size = 16
    lane = lax.broadcasted_iota(jnp.int32, (size, LANES), 1)
    sub = lax.broadcasted_iota(jnp.int32, (size, LANES), 0)

    def row(x, j):
        return jnp.broadcast_to(x[j : j + 1, :], (size, LANES))

    def blocks(first, last):
        low = first * size
        lane_all = lax.broadcasted_iota(jnp.int32, (rank - low, LANES), 1)

        def block(b, _):
            rows = pl.ds(pl.multiple_of(b * size, size), size)
            a = a_ref[low:rank, :]
            r = a_ref[rows, :]
            cols = [jnp.broadcast_to(r[:, k : k + 1], (size, LANES)) for k in range(size)]
            q = jnp.where(lane < size, 0.0, r)
            v = jnp.zeros((size, LANES), jnp.float32)
            pivots = jnp.zeros((size, LANES), jnp.float32)
            inverses = jnp.zeros((size, LANES), jnp.float32)
            for j in range(size):
                pivot = row(cols[j], j)
                inv = 1.0 / pivot
                here = sub == j
                m = jnp.where(here, 0.0, cols[j] * inv)
                qj = row(q, j) + jnp.where(lane == j, 1.0, 0.0)
                pivots = jnp.where(here, pivot, pivots)
                inverses = jnp.where(here, inv, inverses)
                v = jnp.where(here, qj, v)
                q = jnp.where(here, qj, q - m * qj)
                for k in range(j + 1, size):
                    cols[k] = cols[k] - m * row(cols[k], j)
            q = q * inverses
            total = jnp.zeros((rank - low, LANES), jnp.float32)
            for k in range(size):
                total = total + a[:, k : k + 1] * q[k : k + 1, :]
            a_ref[low:rank, :] = pltpu.roll(jnp.where(lane_all < size, 0.0, a) - total, LANES - size, 1)
            v = pltpu.roll(v * lax.rsqrt(pivots), b * size, 1)
            out_ref[rows, :] = jnp.where(lane < (b + 1) * size, v, 0.0)
            return 0

        lax.fori_loop(first, last, block, 0)

    quarter = rank // size // 4
    for i in range(4):
        blocks(i * quarter, (i + 1) * quarter)


FAR = [(dy, dx) for dy in (2, 1, 3, 0) for dx in (2, 1, 3, 0) if (dy, dx) != (0, 0)]
NEAR = sorted(FAR, key=lambda d: min(d[0], 4 - d[0]) + min(d[1], 4 - d[1]))
W_ORDER, G_ORDER, F_ORDER, S_ORDER = NEAR, FAR, FAR, FAR


def main_kernel(
    grad, mom, qprev, factor, ortho, sq, buf,
    gbuf, mbuf, qbuf, bb, pp, prs, pw, pt, p2, gh, cg, gx, gs, amat, lmat, wt, wc, wr, fb, sz, sx,
    in_sem, s1, r1, s2, r2, s3, r3, s4, r4, s5, r5, s6, r6, s7, r7, s8, r8, s9, r9, sf, s10, r10,
):
    rowi = lax.axis_index("row")
    c = lax.axis_index("col")
    chip = rowi // 2
    k = lax.rem(rowi, 2)
    other = 1 - k
    sibling = (chip * 2 + other, c)
    tiles = bb.shape[1] // LANES
    share = wr.shape[1]

    def zpeer(o):
        t = lax.rem(c + o, Z)
        return t, (rowi, t)

    def zother(o):
        return (chip * 2 + other, lax.rem(c + o, Z))

    def cpeer(d):
        t = lax.rem(chip // 4 + d[0], 4) * 4 + lax.rem(chip + d[1], 4)
        return t, (t * 2 + k, c)

    others = [cpeer(d) for d in NEAR]
    w_others = [cpeer(d) for d in W_ORDER]
    g_others = [cpeer(d) for d in G_ORDER]
    f_others = [cpeer(d) for d in F_ORDER]
    s_others = [cpeer(d) for d in S_ORDER]

    far_first = (4, 3, 5, 2, 6, 1, 7)
    barrier = pltpu.get_barrier_semaphore()

    for o in far_first:
        pl.semaphore_signal(barrier, inc=1, device_id=zpeer(o)[1], device_id_type=MESH)
    for o in far_first:
        pl.semaphore_signal(barrier, inc=1, device_id=zother(o), device_id_type=MESH)
    for _, dev in others:
        pl.semaphore_signal(barrier, inc=1, device_id=dev, device_id_type=MESH)
    pl.semaphore_signal(barrier, inc=1, device_id=sibling, device_id_type=MESH)

    bounds = [0, 7, 14, 20, tiles]
    loads = []
    for i in range(4):
        lanes = pl.ds(bounds[i] * LANES, (bounds[i + 1] - bounds[i]) * LANES)
        part = [
            pltpu.make_async_copy(grad.at[:, lanes], gbuf.at[:, lanes], in_sem.at[i, 0]),
            pltpu.make_async_copy(mom.at[:, lanes], mbuf.at[:, lanes], in_sem.at[i, 1]),
            pltpu.make_async_copy(qprev.at[lanes, :], qbuf.at[lanes, :], in_sem.at[i, 2]),
        ]
        for copy in part:
            copy.start()
        loads.append(part)

    rows = bb.shape[0]
    for i in range(4):
        for copy in loads[i]:
            copy.wait()
        lanes = pl.ds(bounds[i] * LANES, (bounds[i + 1] - bounds[i]) * LANES)

        def strip(s, _):
            rs = pl.ds(pl.multiple_of(s * 32, 32), 32)
            g = gbuf[rs, lanes].astype(jnp.float32)
            m = mbuf[rs, lanes].astype(jnp.float32)
            b = momentum_keep * m + g
            buf[rs, lanes] = b
            bb[rs, lanes] = b.astype(jnp.bfloat16)
            return 0

        lax.fori_loop(0, rows // 32, strip, 0)
        d = jnp.dot(bb[:, lanes], qbuf[lanes, :].astype(jnp.bfloat16), preferred_element_type=jnp.float32)
        d = d.reshape(Z, rows // Z, LANES)
        pp[...] = d if i == 0 else pp[...] + d

    pl.semaphore_wait(barrier, 2 * (Z - 1) + CHIPS - 1 + 1)

    sends, late = [], []

    def drain(copies):
        for copy in copies:
            copy.wait_send()
        copies.clear()

    for o in far_first:
        t, dev = zpeer(o)
        copy = remote(pp.at[t], prs.at[c], s1.at[o], r1.at[c], dev)
        copy.start()
        sends.append(copy)
    red = pp[c]
    for o in (1, 7, 2, 6, 3, 5, 4):
        s = lax.rem(c + o, Z)
        remote(pp.at[s], prs.at[s], s1.at[0], r1.at[s], sibling).wait_recv()
        red = red + prs[s]
    pw[c] = red
    for o in far_first:
        t, dev = zpeer(o)
        copy = remote(pw.at[c], pw.at[c], s2.at[o], r2.at[c], dev)
        copy.start()
        sends.append(copy)
    for o in (1, 7, 2, 6, 3, 5, 4):
        s = lax.rem(c + o, Z)
        remote(pw.at[s], pw.at[s], s2.at[0], r2.at[s], sibling).wait_recv()

    power = pw[...].reshape(rows, LANES)
    hi = power.astype(jnp.bfloat16)
    p2[:, 0:128] = hi
    p2[:, 128:256] = (power - hi.astype(jnp.float32)).astype(jnp.bfloat16)
    for start, stop in ((0, bb.shape[1] // 2), (bb.shape[1] // 2, bb.shape[1])):
        d = lax.dot_general(
            bb[:, start:stop], p2[...], (((0,), (0,)), ((), ())), preferred_element_type=jnp.float32
        )
        d = d[:, 0:128] + d[:, 128:256]
        for place in range(start // share, -(-stop // share)):
            a, b = max(start, place * share), min(stop, (place + 1) * share)
            wt[place // 2, place % 2, a - place * share : b - place * share, :] = d[a - start : b - start]

    def exchange(u):
        return remote(wt.at[u, other], wc.at[u], s4.at[u], r4.at[u], sibling)

    for u, _ in w_others:
        exchange(u).start()
    exchange(chip).start()

    pt[...] = power.T
    part = pt[pl.ds(pl.multiple_of(c * 16, 16), 16), :]
    part = jnp.dot(part, power, precision=HIGHEST, preferred_element_type=jnp.float32)
    gh[...] = part.reshape(2, 8, LANES)
    copy = remote(gh.at[other], cg, s3, r3, sibling)
    copy.start()
    sends.append(copy)

    remote(cg, cg, s3, r3, sibling).wait_recv()
    gx[chip] = gh[k] + cg[...]
    for i, (t, dev) in enumerate(g_others):
        copy = remote(gx.at[chip], gx.at[chip], s5.at[i], r5.at[chip], dev)
        copy.start()
        sends.append(copy)

    for i, (u, dev) in enumerate(w_others):
        exchange(u).wait_recv()
        wc[u] = wc[u] + wt[u, k]
        copy = remote(wc.at[u], wr.at[chip], s6.at[i], r6.at[chip], dev)
        copy.start()
        late.append(copy)
    exchange(chip).wait_recv()
    wr[chip] = wc[chip] + wt[chip, k]

    for s, _ in others:
        remote(gx.at[s], gx.at[s], s5.at[0], r5.at[s], sibling).wait_recv()
    total = gx[0]
    for s in range(1, CHIPS):
        total = total + gx[s]
    eight = 2 * c + k

    def spread(ref, send, recv, sends):
        for o in far_first:
            for core, dev in enumerate((zpeer(o)[1], zother(o))):
                copy = remote(ref.at[eight], ref.at[eight], send.at[core, o], recv.at[eight], dev)
                copy.start()
                sends.append(copy)
        copy = remote(ref.at[eight], ref.at[eight], send.at[0, 0], recv.at[eight], sibling)
        copy.start()
        sends.append(copy)

    def collect(ref, send, recv):
        for o in (0, 1, 7, 2, 6, 3, 5, 4):
            for core in (other,) if o == 0 else (k, other):
                s = 2 * lax.rem(c + o, Z) + core
                remote(ref.at[s], ref.at[s], send.at[0, 0], recv.at[s], sibling).wait_recv()

    gs[eight] = total
    early = sends
    sends = late
    spread(gs, s7, r7, sends)
    drain(early)
    for t in range(CHIPS):
        exchange(t).wait_send()
    collect(gs, s7, r7)
    amat[...] = gs[...].reshape(LANES, LANES)

    inverse_cholesky(amat, lmat)
    linv = lmat[...]

    slot = chip * 2 + k
    for s, _ in others:
        remote(wr.at[s], wr.at[s], s6.at[0], r6.at[s], sibling).wait_recv()
    w = wr[0]
    for s in range(1, CHIPS):
        w = w + wr[s]
    f = lax.dot_general(w, linv, (((1,), (1,)), ((), ())), precision=HIGHEST, preferred_element_type=jnp.float32)
    fb[slot] = jnp.concatenate([f, jnp.zeros((fb.shape[1] - share, LANES), jnp.float32)], axis=0).astype(jnp.bfloat16)
    shared = []
    for i, (t, dev) in enumerate(f_others):
        copy = remote(fb.at[slot], fb.at[slot], s8.at[i], r8.at[slot], dev)
        copy.start()
        shared.append(copy)

    sz[eight] = jnp.broadcast_to(jnp.sum(f * f, axis=0, keepdims=True), (8, LANES))
    early, sends = sends, []
    spread(sz, s9, r9, sends)
    def forward(t):
        place = t * 2 + k
        return remote(fb.at[place], fb.at[place], sf.at[t], r8.at[place], sibling)

    forward(chip).start()
    ortho[...] = lax.dot_general(
        pw[...].reshape(rows, LANES), linv, (((1,), (1,)), ((), ())), precision=HIGHEST, preferred_element_type=jnp.float32
    ).astype(jnp.bfloat16)
    drain(early)
    collect(sz, s9, r9)
    tot = sz[0]
    for s in range(1, 2 * Z):
        tot = tot + sz[s]
    sx[chip] = tot

    last = []
    for i, (t, dev) in enumerate(s_others):
        copy = remote(sx.at[chip], sx.at[chip], s10.at[i], r10.at[chip], dev)
        copy.start()
        last.append(copy)

    drain(sends)
    for t, _ in f_others:
        forward(t).wait_recv()
        forward(t).start()
    drain(shared)
    for s, _ in others:
        remote(sx.at[s], sx.at[s], s10.at[0], r10.at[s], sibling).wait_recv()
    tot = sx[0]
    for s in range(1, CHIPS):
        tot = tot + sx[s]
    sq[...] = tot

    for t in range(CHIPS):
        place = t * 2 + other
        remote(fb.at[place], fb.at[place], sf.at[t], r8.at[place], sibling).wait_recv()
    for i in range(2 * CHIPS):
        factor[i * share : (i + 1) * share, :] = fb[i, 0:share].astype(jnp.float32)
    drain(last)
    for t in range(CHIPS):
        forward(t).wait_send()


def final_kernel(scaling, factor, ortho, sq, buf, mout, direction, qnew, mbuf, dbuf, qbuf, sem):
    inv = 1.0 / jnp.sqrt(sq[0:1] + epsilon)
    o = ortho[...]
    steps = factor.shape[0] // (2 * LANES)
    copies = []

    def times(x):
        return lax.dot_general(
            o, x.astype(jnp.bfloat16), (((1,), (1,)), ((), ())), preferred_element_type=jnp.float32
        )

    for part, (first, last) in enumerate(((0, 1), (1, 4), (4, 8), (8, steps))):
        cols = slice(first * 2 * LANES, last * 2 * LANES)
        for u in range(first, last):
            c = slice(2 * u * LANES, 2 * (u + 1) * LANES)
            q = factor[c, :] * inv
            qbuf[c, :] = q
            dbuf[:, c] = (scaling * times(q)).astype(jnp.bfloat16)
            mbuf[:, c] = (buf[:, c] - (1.0 - momentum_keep) * times(factor[c, :])).astype(jnp.bfloat16)
        pairs = (
            (qbuf.at[cols, :], qnew.at[cols, :]),
            (dbuf.at[:, cols], direction.at[:, cols]),
            (mbuf.at[:, cols], mout.at[:, cols]),
        )
        for n, (src, dst) in enumerate(pairs):
            copy = pltpu.make_async_copy(src, dst, sem.at[part, n])
            copy.start()
            copies.append(copy)
    for copy in copies:
        copy.wait()


def per_device(grad, momentum, q_prev):
    rows, cols = grad.shape
    share = cols // (2 * CHIPS)
    f32, bf16 = jnp.float32, jnp.bfloat16
    dma = pltpu.SemaphoreType.DMA
    vmem = pl.BlockSpec(memory_space=pltpu.VMEM)
    hbm = pl.BlockSpec(memory_space=pltpu.HBM)
    factor, ortho, sq, buffer = pl.pallas_call(
        main_kernel,
        out_shape=(
            jax.ShapeDtypeStruct((cols, LANES), f32),
            jax.ShapeDtypeStruct((rows, LANES), bf16),
            jax.ShapeDtypeStruct((8, LANES), f32),
            jax.ShapeDtypeStruct((rows, cols), f32),
        ),
        in_specs=[hbm] * 3,
        out_specs=(vmem,) * 4,
        scratch_shapes=[
            pltpu.VMEM((rows, cols), bf16),
            pltpu.VMEM((rows, cols), bf16),
            pltpu.VMEM((cols, LANES), f32),
            pltpu.VMEM((rows, cols), bf16),
            pltpu.VMEM((Z, rows // Z, LANES), f32),
            pltpu.VMEM((Z, rows // Z, LANES), f32),
            pltpu.VMEM((Z, rows // Z, LANES), f32),
            pltpu.VMEM((LANES, rows), f32),
            pltpu.VMEM((rows, 2 * LANES), bf16),
            pltpu.VMEM((2, 8, LANES), f32),
            pltpu.VMEM((8, LANES), f32),
            pltpu.VMEM((CHIPS, 8, LANES), f32),
            pltpu.VMEM((2 * Z, 8, LANES), f32),
            pltpu.VMEM((LANES, LANES), f32),
            pltpu.VMEM((LANES, LANES), f32),
            pltpu.VMEM((CHIPS, 2, share, LANES), f32),
            pltpu.VMEM((CHIPS, share, LANES), f32),
            pltpu.VMEM((CHIPS, share, LANES), f32),
            pltpu.VMEM((2 * CHIPS, -(-share // 16) * 16, LANES), bf16),
            pltpu.VMEM((2 * Z, 8, LANES), f32),
            pltpu.VMEM((CHIPS, 8, LANES), f32),
            dma((4, 3)),
            dma((Z,)), dma((Z,)),
            dma((Z,)), dma((Z,)),
            dma, dma,
            dma((CHIPS,)), dma((CHIPS,)),
            dma((CHIPS,)), dma((CHIPS,)),
            dma((CHIPS,)), dma((CHIPS,)),
            dma((2, Z)), dma((2 * Z,)),
            dma((CHIPS,)), dma((2 * CHIPS,)),
            dma((2, Z)), dma((2 * Z,)),
            dma((CHIPS,)),
            dma((CHIPS,)), dma((CHIPS,)),
        ],
        compiler_params=pltpu.CompilerParams(
            collective_id=0, has_side_effects=True, vmem_limit_bytes=40 * 2**20
        ),
        name="power_gram_factor",
    )(*(pltpu.with_memory_space_constraint(x, pltpu.HBM) for x in (grad, momentum, q_prev)))

    total_rows = rows * lax.axis_size("row")
    total_cols = cols * lax.axis_size("col")
    scaling = math.sqrt(total_rows * total_cols / q_prev.shape[1])
    return pl.pallas_call(
        functools.partial(final_kernel, scaling),
        out_shape=(
            jax.ShapeDtypeStruct((rows, cols), bf16),
            jax.ShapeDtypeStruct((rows, cols), bf16),
            jax.ShapeDtypeStruct((cols, LANES), f32),
        ),
        in_specs=[vmem] * 4,
        out_specs=(hbm,) * 3,
        scratch_shapes=[
            pltpu.VMEM((rows, cols), bf16),
            pltpu.VMEM((rows, cols), bf16),
            pltpu.VMEM((cols, LANES), f32),
            dma((4, 3)),
        ],
        compiler_params=pltpu.CompilerParams(vmem_limit_bytes=24 * 2**20),
        name="outputs",
    )(factor, ortho, sq, buffer)


def solution(mesh):
    return jax.shard_map(
        per_device,
        mesh=mesh,
        in_specs=(P("row", "col"), P("row", "col"), P("col", None)),
        out_specs=(P("row", "col"), P("row", "col"), P("col", None)),
        check_vma=False,
    )
```

```python
import functools
import math

import jax
import jax.numpy as jnp
from jax import lax
from jax.experimental import pallas as pl
from jax.experimental.pallas import tpu as pltpu
from jax.sharding import PartitionSpec as P

momentum_keep = 0.9
epsilon = 1e-06
MESH = pl.DeviceIdType.MESH
HIGHEST = lax.Precision.HIGHEST
LANES = 128
Z = 8
CHIPS = 16


def remote(src, dst, send, recv, device):
    return pltpu.make_async_remote_copy(
        src_ref=src, dst_ref=dst, send_sem=send, recv_sem=recv, device_id=device, device_id_type=MESH
    )


def inverse_cholesky(a_ref, out_ref):
    rank = a_ref.shape[0]
    size = 16
    lane = lax.broadcasted_iota(jnp.int32, (size, LANES), 1)
    sub = lax.broadcasted_iota(jnp.int32, (size, LANES), 0)

    def row(x, j):
        return jnp.broadcast_to(x[j : j + 1, :], (size, LANES))

    def blocks(first, last):
        low = first * size
        lane_all = lax.broadcasted_iota(jnp.int32, (rank - low, LANES), 1)

        def block(b, _):
            rows = pl.ds(pl.multiple_of(b * size, size), size)
            a = a_ref[low:rank, :]
            r = a_ref[rows, :]
            cols = [jnp.broadcast_to(r[:, k : k + 1], (size, LANES)) for k in range(size)]
            q = jnp.where(lane < size, 0.0, r)
            v = jnp.zeros((size, LANES), jnp.float32)
            pivots = jnp.zeros((size, LANES), jnp.float32)
            inverses = jnp.zeros((size, LANES), jnp.float32)
            for j in range(size):
                pivot = row(cols[j], j)
                inv = 1.0 / pivot
                here = sub == j
                m = jnp.where(here, 0.0, cols[j] * inv)
                qj = row(q, j) + jnp.where(lane == j, 1.0, 0.0)
                pivots = jnp.where(here, pivot, pivots)
                inverses = jnp.where(here, inv, inverses)
                v = jnp.where(here, qj, v)
                q = jnp.where(here, qj, q - m * qj)
                for k in range(j + 1, size):
                    cols[k] = cols[k] - m * row(cols[k], j)
            q = q * inverses
            total = jnp.zeros((rank - low, LANES), jnp.float32)
            for k in range(size):
                total = total + a[:, k : k + 1] * q[k : k + 1, :]
            a_ref[low:rank, :] = pltpu.roll(jnp.where(lane_all < size, 0.0, a) - total, LANES - size, 1)
            v = pltpu.roll(v * lax.rsqrt(pivots), b * size, 1)
            out_ref[rows, :] = jnp.where(lane < (b + 1) * size, v, 0.0)
            return 0

        lax.fori_loop(first, last, block, 0)

    quarter = rank // size // 4
    for i in range(4):
        blocks(i * quarter, (i + 1) * quarter)


FAR = [(dy, dx) for dy in (2, 1, 3, 0) for dx in (2, 1, 3, 0) if (dy, dx) != (0, 0)]
NEAR = sorted(FAR, key=lambda d: min(d[0], 4 - d[0]) + min(d[1], 4 - d[1]))
W_ORDER, G_ORDER, F_ORDER, S_ORDER = NEAR, FAR, FAR, FAR


def main_kernel(
    grad, mom, qprev, factor, ortho, sq, buf,
    gbuf, mbuf, qbuf, bb, pp, prs, pw, pt, p2, gh, cg, gx, gs, amat, lmat, wt, wc, wr, fb, sz, sx,
    in_sem, s1, r1, s2, r2, s3, r3, s4, r4, s5, r5, s6, r6, s7, r7, s8, r8, s9, r9, sf, s10, r10,
):
    rowi = lax.axis_index("row")
    c = lax.axis_index("col")
    chip = rowi // 2
    k = lax.rem(rowi, 2)
    other = 1 - k
    sibling = (chip * 2 + other, c)
    tiles = bb.shape[1] // LANES
    share = wr.shape[1]

    def zpeer(o):
        t = lax.rem(c + o, Z)
        return t, (rowi, t)

    def zother(o):
        return (chip * 2 + other, lax.rem(c + o, Z))

    def cpeer(d):
        t = lax.rem(chip // 4 + d[0], 4) * 4 + lax.rem(chip + d[1], 4)
        return t, (t * 2 + k, c)

    others = [cpeer(d) for d in NEAR]
    w_others = [cpeer(d) for d in W_ORDER]
    g_others = [cpeer(d) for d in G_ORDER]
    f_others = [cpeer(d) for d in F_ORDER]
    s_others = [cpeer(d) for d in S_ORDER]

    far_first = (4, 3, 5, 2, 6, 1, 7)
    barrier = pltpu.get_barrier_semaphore()

    for o in far_first:
        pl.semaphore_signal(barrier, inc=1, device_id=zpeer(o)[1], device_id_type=MESH)
    for o in far_first:
        pl.semaphore_signal(barrier, inc=1, device_id=zother(o), device_id_type=MESH)
    for _, dev in others:
        pl.semaphore_signal(barrier, inc=1, device_id=dev, device_id_type=MESH)
    pl.semaphore_signal(barrier, inc=1, device_id=sibling, device_id_type=MESH)

    bounds = [0, 8, 15, 21, tiles - 2, tiles]
    loads = []
    for i in range(5):
        lanes = pl.ds(bounds[i] * LANES, (bounds[i + 1] - bounds[i]) * LANES)
        part = [
            pltpu.make_async_copy(grad.at[:, lanes], gbuf.at[:, lanes], in_sem.at[i, 0]),
            pltpu.make_async_copy(mom.at[:, lanes], mbuf.at[:, lanes], in_sem.at[i, 1]),
            pltpu.make_async_copy(qprev.at[lanes, :], qbuf.at[lanes, :], in_sem.at[i, 2]),
        ]
        for copy in part:
            copy.start()
        loads.append(part)

    rows = bb.shape[0]
    for i in range(5):
        for copy in loads[i]:
            copy.wait()
        lanes = pl.ds(bounds[i] * LANES, (bounds[i + 1] - bounds[i]) * LANES)

        def strip(s, _):
            rs = pl.ds(pl.multiple_of(s * 32, 32), 32)
            g = gbuf[rs, lanes].astype(jnp.float32)
            m = mbuf[rs, lanes].astype(jnp.float32)
            b = momentum_keep * m + g
            buf[rs, lanes] = b
            bb[rs, lanes] = b.astype(jnp.bfloat16)
            return 0

        lax.fori_loop(0, rows // 32, strip, 0)
        d = jnp.dot(bb[:, lanes], qbuf[lanes, :].astype(jnp.bfloat16), preferred_element_type=jnp.float32)
        d = d.reshape(Z, rows // Z, LANES)
        pp[...] = d if i == 0 else pp[...] + d

    pl.semaphore_wait(barrier, 2 * (Z - 1) + CHIPS - 1 + 1)

    sends, late = [], []

    def drain(copies):
        for copy in copies:
            copy.wait_send()
        copies.clear()

    for o in far_first:
        t, dev = zpeer(o)
        copy = remote(pp.at[t], prs.at[c], s1.at[o], r1.at[c], dev)
        copy.start()
        sends.append(copy)
    red = pp[c]
    for o in (1, 7, 2, 6, 3, 5, 4):
        s = lax.rem(c + o, Z)
        remote(pp.at[s], prs.at[s], s1.at[0], r1.at[s], sibling).wait_recv()
        red = red + prs[s]
    pw[c] = red
    for o in far_first:
        t, dev = zpeer(o)
        copy = remote(pw.at[c], pw.at[c], s2.at[o], r2.at[c], dev)
        copy.start()
        sends.append(copy)
    for o in (1, 7, 2, 6, 3, 5, 4):
        s = lax.rem(c + o, Z)
        remote(pw.at[s], pw.at[s], s2.at[0], r2.at[s], sibling).wait_recv()

    power = pw[...].reshape(rows, LANES)
    hi = power.astype(jnp.bfloat16)
    p2[:, 0:128] = hi
    p2[:, 128:256] = (power - hi.astype(jnp.float32)).astype(jnp.bfloat16)
    for i in range(5):
        start, stop = bounds[i] * LANES, bounds[i + 1] * LANES
        d = lax.dot_general(
            bb[:, start:stop], p2[...], (((0,), (0,)), ((), ())), preferred_element_type=jnp.float32
        )
        d = d[:, 0:128] + d[:, 128:256]
        for place in range(start // share, -(-stop // share)):
            a, b = max(start, place * share), min(stop, (place + 1) * share)
            wt[place // 2, place % 2, a - place * share : b - place * share, :] = d[a - start : b - start]

    def exchange(u):
        return remote(wt.at[u, other], wc.at[u], s4.at[u], r4.at[u], sibling)

    for u, _ in w_others:
        exchange(u).start()
    exchange(chip).start()

    pt[...] = power.T
    part = pt[pl.ds(pl.multiple_of(c * 16, 16), 16), :]
    part = jnp.dot(part, power, precision=HIGHEST, preferred_element_type=jnp.float32)
    gh[...] = part.reshape(2, 8, LANES)
    copy = remote(gh.at[other], cg, s3, r3, sibling)
    copy.start()
    sends.append(copy)

    remote(cg, cg, s3, r3, sibling).wait_recv()
    gx[chip] = gh[k] + cg[...]
    for i, (t, dev) in enumerate(g_others):
        copy = remote(gx.at[chip], gx.at[chip], s5.at[i], r5.at[chip], dev)
        copy.start()
        sends.append(copy)

    for i, (u, dev) in enumerate(w_others):
        exchange(u).wait_recv()
        wc[u] = wc[u] + wt[u, k]
        copy = remote(wc.at[u], wr.at[chip], s6.at[i], r6.at[chip], dev)
        copy.start()
        late.append(copy)
    exchange(chip).wait_recv()
    wr[chip] = wc[chip] + wt[chip, k]

    for s, _ in others:
        remote(gx.at[s], gx.at[s], s5.at[0], r5.at[s], sibling).wait_recv()
    total = gx[0]
    for s in range(1, CHIPS):
        total = total + gx[s]
    eight = 2 * c + k

    def spread(ref, send, recv, sends):
        for o in far_first:
            for core, dev in enumerate((zpeer(o)[1], zother(o))):
                copy = remote(ref.at[eight], ref.at[eight], send.at[core, o], recv.at[eight], dev)
                copy.start()
                sends.append(copy)
        copy = remote(ref.at[eight], ref.at[eight], send.at[0, 0], recv.at[eight], sibling)
        copy.start()
        sends.append(copy)

    def collect(ref, send, recv):
        for o in (0, 1, 7, 2, 6, 3, 5, 4):
            for core in (other,) if o == 0 else (k, other):
                s = 2 * lax.rem(c + o, Z) + core
                remote(ref.at[s], ref.at[s], send.at[0, 0], recv.at[s], sibling).wait_recv()

    gs[eight] = total
    early = sends
    sends = late
    spread(gs, s7, r7, sends)
    drain(early)
    for t in range(CHIPS):
        exchange(t).wait_send()
    collect(gs, s7, r7)
    amat[...] = gs[...].reshape(LANES, LANES)

    inverse_cholesky(amat, lmat)
    linv = lmat[...]

    slot = chip * 2 + k
    w = wr[chip]
    for s, _ in others:
        remote(wr.at[s], wr.at[s], s6.at[0], r6.at[s], sibling).wait_recv()
        w = w + wr[s]
    f = lax.dot_general(w, linv, (((1,), (1,)), ((), ())), precision=HIGHEST, preferred_element_type=jnp.float32)
    sz[eight] = jnp.broadcast_to(jnp.sum(f * f, axis=0, keepdims=True), (8, LANES))
    early, sends = sends, []
    spread(sz, s9, r9, sends)
    fb[slot] = jnp.concatenate([f, jnp.zeros((fb.shape[1] - share, LANES), jnp.float32)], axis=0).astype(jnp.bfloat16)
    shared = []
    for i, (t, dev) in enumerate(f_others):
        copy = remote(fb.at[slot], fb.at[slot], s8.at[i], r8.at[slot], dev)
        copy.start()
        shared.append(copy)

    def forward(t):
        place = t * 2 + k
        return remote(fb.at[place], fb.at[place], sf.at[t], r8.at[place], sibling)

    forward(chip).start()
    ortho[...] = lax.dot_general(
        pw[...].reshape(rows, LANES), linv, (((1,), (1,)), ((), ())), precision=HIGHEST, preferred_element_type=jnp.float32
    ).astype(jnp.bfloat16)
    drain(early)
    collect(sz, s9, r9)
    tot = sz[0]
    for s in range(1, 2 * Z):
        tot = tot + sz[s]
    sx[chip] = tot

    last = []
    for i, (t, dev) in enumerate(s_others):
        copy = remote(sx.at[chip], sx.at[chip], s10.at[i], r10.at[chip], dev)
        copy.start()
        last.append(copy)

    drain(sends)
    for t, _ in f_others:
        forward(t).wait_recv()
        forward(t).start()
    drain(shared)
    for s, _ in others:
        remote(sx.at[s], sx.at[s], s10.at[0], r10.at[s], sibling).wait_recv()
    tot = sx[0]
    for s in range(1, CHIPS):
        tot = tot + sx[s]
    sq[...] = tot

    for t in range(CHIPS):
        place = t * 2 + other
        remote(fb.at[place], fb.at[place], sf.at[t], r8.at[place], sibling).wait_recv()
    for i in range(2 * CHIPS):
        factor[i * share : (i + 1) * share, :] = fb[i, 0:share].astype(jnp.float32)
    drain(last)
    for t in range(CHIPS):
        forward(t).wait_send()


def final_kernel(scaling, factor, ortho, sq, buf, mout, direction, qnew, mbuf, dbuf, qbuf, sem):
    inv = 1.0 / jnp.sqrt(sq[0:1] + epsilon)
    o = ortho[...]
    steps = factor.shape[0] // (2 * LANES)
    copies = []

    def times(x):
        return lax.dot_general(
            o, x.astype(jnp.bfloat16), (((1,), (1,)), ((), ())), preferred_element_type=jnp.float32
        )

    for part, (first, last) in enumerate(((0, 3), (3, 8), (8, steps))):
        cols = slice(first * 2 * LANES, last * 2 * LANES)
        for u in range(first, last):
            c = slice(2 * u * LANES, 2 * (u + 1) * LANES)
            q = factor[c, :] * inv
            qbuf[c, :] = q
            dbuf[:, c] = (scaling * times(q)).astype(jnp.bfloat16)
            mbuf[:, c] = (buf[:, c] - (1.0 - momentum_keep) * times(factor[c, :])).astype(jnp.bfloat16)
        pairs = (
            (qbuf.at[cols, :], qnew.at[cols, :]),
            (dbuf.at[:, cols], direction.at[:, cols]),
            (mbuf.at[:, cols], mout.at[:, cols]),
        )
        for n, (src, dst) in enumerate(pairs):
            copy = pltpu.make_async_copy(src, dst, sem.at[part, n])
            copy.start()
            copies.append(copy)
    for copy in copies:
        copy.wait()


def per_device(grad, momentum, q_prev):
    rows, cols = grad.shape
    share = cols // (2 * CHIPS)
    f32, bf16 = jnp.float32, jnp.bfloat16
    dma = pltpu.SemaphoreType.DMA
    vmem = pl.BlockSpec(memory_space=pltpu.VMEM)
    hbm = pl.BlockSpec(memory_space=pltpu.HBM)
    factor, ortho, sq, buffer = pl.pallas_call(
        main_kernel,
        out_shape=(
            jax.ShapeDtypeStruct((cols, LANES), f32),
            jax.ShapeDtypeStruct((rows, LANES), bf16),
            jax.ShapeDtypeStruct((8, LANES), f32),
            jax.ShapeDtypeStruct((rows, cols), f32),
        ),
        in_specs=[hbm] * 3,
        out_specs=(vmem,) * 4,
        scratch_shapes=[
            pltpu.VMEM((rows, cols), bf16),
            pltpu.VMEM((rows, cols), bf16),
            pltpu.VMEM((cols, LANES), f32),
            pltpu.VMEM((rows, cols), bf16),
            pltpu.VMEM((Z, rows // Z, LANES), f32),
            pltpu.VMEM((Z, rows // Z, LANES), f32),
            pltpu.VMEM((Z, rows // Z, LANES), f32),
            pltpu.VMEM((LANES, rows), f32),
            pltpu.VMEM((rows, 2 * LANES), bf16),
            pltpu.VMEM((2, 8, LANES), f32),
            pltpu.VMEM((8, LANES), f32),
            pltpu.VMEM((CHIPS, 8, LANES), f32),
            pltpu.VMEM((2 * Z, 8, LANES), f32),
            pltpu.VMEM((LANES, LANES), f32),
            pltpu.VMEM((LANES, LANES), f32),
            pltpu.VMEM((CHIPS, 2, share, LANES), f32),
            pltpu.VMEM((CHIPS, share, LANES), f32),
            pltpu.VMEM((CHIPS, share, LANES), f32),
            pltpu.VMEM((2 * CHIPS, -(-share // 16) * 16, LANES), bf16),
            pltpu.VMEM((2 * Z, 8, LANES), f32),
            pltpu.VMEM((CHIPS, 8, LANES), f32),
            dma((5, 3)),
            dma((Z,)), dma((Z,)),
            dma((Z,)), dma((Z,)),
            dma, dma,
            dma((CHIPS,)), dma((CHIPS,)),
            dma((CHIPS,)), dma((CHIPS,)),
            dma((CHIPS,)), dma((CHIPS,)),
            dma((2, Z)), dma((2 * Z,)),
            dma((CHIPS,)), dma((2 * CHIPS,)),
            dma((2, Z)), dma((2 * Z,)),
            dma((CHIPS,)),
            dma((CHIPS,)), dma((CHIPS,)),
        ],
        compiler_params=pltpu.CompilerParams(
            collective_id=0, has_side_effects=True, vmem_limit_bytes=40 * 2**20
        ),
        name="power_gram_factor",
    )(*(pltpu.with_memory_space_constraint(x, pltpu.HBM) for x in (grad, momentum, q_prev)))

    total_rows = rows * lax.axis_size("row")
    total_cols = cols * lax.axis_size("col")
    scaling = math.sqrt(total_rows * total_cols / q_prev.shape[1])
    return pl.pallas_call(
        functools.partial(final_kernel, scaling),
        out_shape=(
            jax.ShapeDtypeStruct((rows, cols), bf16),
            jax.ShapeDtypeStruct((rows, cols), bf16),
            jax.ShapeDtypeStruct((cols, LANES), f32),
        ),
        in_specs=[vmem] * 4,
        out_specs=(hbm,) * 3,
        scratch_shapes=[
            pltpu.VMEM((rows, cols), bf16),
            pltpu.VMEM((rows, cols), bf16),
            pltpu.VMEM((cols, LANES), f32),
            dma((3, 3)),
        ],
        compiler_params=pltpu.CompilerParams(vmem_limit_bytes=24 * 2**20),
        name="outputs",
    )(factor, ortho, sq, buffer)


def solution(mesh):
    return jax.shard_map(
        per_device,
        mesh=mesh,
        in_specs=(P("row", "col"), P("row", "col"), P("col", None)),
        out_specs=(P("row", "col"), P("row", "col"), P("col", None)),
        check_vma=False,
    )
```
